1024 devices in a mesh: gx: 32 (over x, y_lo, core), gy: 4 (over y_hi), gz: 8 (over z).
Axes of the slice: x: 8, y: 8 (y_hi: 4, y_lo: 2; y = y_hi * 2 + y_lo), z: 8, core: 2. Of those that a mesh axis runs over, the one named last changes fastest.
Arguments:
- features: bfloat16 [32, 4, 8, 128, 128], P('gx', 'gy', 'gz'), may hold values from -6 to 6
- positions: bfloat16 [32, 4, 8, 3, 128], P('gx', 'gy', 'gz'), may hold values from 0 to 1
- neighbour_ids: int32 [32, 4, 8, 32, 128], P('gx', 'gy', 'gz'), may hold values from 0 to 3455, as said below
- neighbour_counts: int32 [32, 4, 8, 128], P('gx', 'gy', 'gz'), may hold values from 8 to 32, as said below
- radial_weight: float32 [8, 384], replicated, may hold values from -2 to 2
- mix_weight: float32 [3, 128, 128], replicated, may hold values from -0.5 to 0.5
- readout_weight: float32 [384, 16], replicated, may hold values from -0.3125 to 0.3125
- readout_vector: float32 [16], replicated, may hold values from -1.5 to 1.5
- self_weight: float32 [128], replicated, may hold values from -0.5 to 0.5
Outputs:
- atom_energy: float32 [32, 4, 8, 128], P('gx', 'gy', 'gz')
- forces: float32 [32, 4, 8, 3, 128], P('gx', 'gy', 'gz')
The draws below stay inside these ranges and needn't reach their ends.
Inputs may be any that keep to these rules, and one draw needn't show every extreme that they name: `neighbour_ids`: entry n names slot n % 128 of one of the 27 bins around the atom's bin (offset from n // 128 as in the reference program), never the atom itself; the same neighbour may appear twice. `neighbour_counts`: in every bin some atom has exactly 32 live neighbour slots.
All inputs are finite; a program needn't handle non-finite values.
Results may differ from the reference program's by a relative error of at most 0.0008.
Values may be sent and summed in bfloat16 or wider, within the bound.
A program may use at most 32 MiB of HBM per device.

```python
import math
import jax
import jax.numpy as jnp
import numpy as np
from jax import lax

CHANNELS = 128
ATOMS_BIN = 128
NEIGHBOURS = 32
RADIAL_BASIS = 8
READOUT = 16
GRID_X = 32
GRID_Y = 4
GRID_Z = 8


def draw_neighbour_ids(key, part):
    key = jax.random.fold_in(key, 5)
    array_shape = (GRID_X, GRID_Y, GRID_Z, NEIGHBOURS, ATOMS_BIN)
    drawn = jax.random.randint(key, array_shape, 0, 27 * ATOMS_BIN - 1)
    slot_index = lax.broadcasted_iota(jnp.int32, array_shape, 4)
    itself = 13 * ATOMS_BIN + slot_index
    return jnp.where(drawn >= itself, drawn + 1, drawn).astype(jnp.int32)


def draw_neighbour_counts(key, part):
    key = jax.random.fold_in(key, 9)
    key_base, key_full = jax.random.split(key)
    array_shape = (GRID_X, GRID_Y, GRID_Z, ATOMS_BIN)
    base_count = jax.random.randint(key_base, array_shape, NEIGHBOURS // 4, NEIGHBOURS + 1)
    chosen = jax.random.randint(key_full, (GRID_X, GRID_Y, GRID_Z, 1), 0, ATOMS_BIN)
    slot_index = lax.broadcasted_iota(jnp.int32, array_shape, 3)
    return jnp.where(slot_index == chosen, NEIGHBOURS, base_count).astype(jnp.int32)


def level_of(stream_key, shape, cuts, low, high):
    def one(axis_at, blocks):
        draws = jax.random.uniform(jax.random.fold_in(jax.random.fold_in(stream_key, 6), axis_at), (blocks,), jnp.float32, low / len(cuts), high / len(cuts))
        return jnp.repeat(jnp.exp(draws), shape[axis_at] // blocks).reshape((-1,) + (1,) * (len(shape) - axis_at - 1))

    gain = one(*cuts[0])
    for cut in cuts[1:]:
        gain = gain * one(*cut)
    return gain


def normal_values(key, extent, width, bound, shards=(), kind=jnp.bfloat16):
    values = width * jax.random.normal(key, extent, jnp.float32)
    if shards:
        values = values * level_of(key, extent, shards, -0.22, 0.18)
    return jnp.clip(values, -bound, bound).astype(kind)


def setup_inputs(seed: int = 0) -> dict:
    key_of = jax.random.split(jax.random.key(seed), 10)
    return {
        "features": normal_values(key_of[0], (GRID_X, GRID_Y, GRID_Z, ATOMS_BIN, CHANNELS), 1.0, 6.0, ((0, 32), (1, 4), (2, 8))),
        "positions": jnp.clip(1.0 * jax.random.uniform(key_of[1], (GRID_X, GRID_Y, GRID_Z, 3, ATOMS_BIN), jnp.float32) ** level_of(key_of[1], (GRID_X, GRID_Y, GRID_Z, 3, ATOMS_BIN), ((0, 32), (1, 4), (2, 8)), -0.2, 0.2), 0.0, 1.0).astype(jnp.bfloat16),
        "neighbour_ids": draw_neighbour_ids(jax.random.fold_in(key_of[9], 71), 0),
        "neighbour_counts": draw_neighbour_counts(jax.random.fold_in(key_of[9], 71), 0),
        "radial_weight": normal_values(key_of[4], (RADIAL_BASIS, 3 * CHANNELS), RADIAL_BASIS ** -0.5, 2.0, (), jnp.float32),
        "mix_weight": normal_values(key_of[5], (3, CHANNELS, CHANNELS), CHANNELS ** -0.5, 0.5, (), jnp.float32),
        "readout_weight": normal_values(key_of[6], (3 * CHANNELS, READOUT), (3 * CHANNELS) ** -0.5, 0.3125, (), jnp.float32),
        "readout_vector": normal_values(key_of[7], (READOUT,), READOUT ** -0.5, 1.5, (), jnp.float32),
        "self_weight": normal_values(key_of[8], (CHANNELS,), CHANNELS ** -0.5, 0.5, (), jnp.float32),
    }


highest_precision = lax.Precision.HIGHEST
degree_table = np.array([0, 1, 1, 1, 2, 2, 2, 2, 2])

def offsets_table(atom_count):
    bin_number = jnp.arange(27 * atom_count, dtype=jnp.int32) // atom_count
    return jnp.stack([bin_number // 9 - 1, bin_number // 3 % 3 - 1, bin_number % 3 - 1]).astype(jnp.float32)

def harmonics(across, along, upward, square):
    root_three = math.sqrt(3.0)
    root_fifteen = math.sqrt(15.0)
    root_five = math.sqrt(5.0)
    return jnp.stack([jnp.ones_like(square), root_three * across, root_three * along, root_three * upward, root_fifteen * across * along, root_fifteen * along * upward, 0.5 * root_five * (3.0 * upward * upward - square), root_fifteen * across * upward, 0.5 * root_fifteen * (across * across - along * along)])

def bin_energy(block_feat, block_pos, bin_ids, bin_counts, radial_weight, mix_weight, readout_weight, readout_vector, self_weight):
    slot_count, atom_count = bin_ids.shape
    channel_count = block_feat.shape[1]
    basis_count = radial_weight.shape[0]
    shifted = block_pos + offsets_table(atom_count)
    centre = block_pos[:, 13 * atom_count:14 * atom_count]
    relative = jnp.take(shifted, bin_ids, axis=1) - centre[:, None, :]
    square = relative[0] * relative[0] + relative[1] * relative[1] + relative[2] * relative[2]
    envelope = (1.0 - square / 16.0) * (1.0 - square / 16.0)
    live_mask = (lax.broadcasted_iota(jnp.int32, (slot_count, atom_count), 0) < bin_counts[None, :]).astype(jnp.float32)
    decay_rates = 0.08 * 2.0 ** jnp.arange(basis_count, dtype=jnp.float32)
    radial = jnp.exp(-decay_rates[:, None, None] * square[None]) * (envelope * live_mask)[None]
    angular = harmonics(relative[0], relative[1], relative[2], square)
    edge_weights = (radial[:, None] * angular[None]).reshape(basis_count * 9, slot_count, atom_count)
    gathered = jnp.take(block_feat, bin_ids, axis=0).astype(jnp.float32)
    projected = jnp.einsum('qka,kac->qac', edge_weights, gathered, precision=highest_precision)
    projected = projected.reshape(basis_count, 9, atom_count, channel_count)
    per_order = radial_weight.reshape(basis_count, 3, channel_count)[:, degree_table]
    amplitude = 0.25 * jnp.einsum('nmac,nmc->mac', projected, per_order, precision=highest_precision)
    mixed_feats = jnp.einsum('mac,mcd->mad', amplitude, mix_weight[degree_table], precision=highest_precision)
    invariants = jnp.concatenate([mixed_feats[0], lax.optimization_barrier(jnp.sum(mixed_feats[1:4] * mixed_feats[1:4], axis=0)), lax.optimization_barrier(jnp.sum(mixed_feats[4:9] * mixed_feats[4:9], axis=0))], axis=1)
    hidden = jax.nn.silu(jnp.dot(invariants, readout_weight, precision=highest_precision))
    own_feat = block_feat[13 * atom_count:14 * atom_count].astype(jnp.float32)
    return jnp.dot(hidden, readout_vector, precision=highest_precision) + jnp.dot(own_feat, self_weight, precision=highest_precision)

def grid_energies(pad_feat, pad_pos, neighbour_ids, neighbour_counts, radial_weight, mix_weight, readout_weight, readout_vector, self_weight):
    count_x, count_y, count_z, slot_count, atom_count = neighbour_ids.shape
    channel_count = pad_feat.shape[4]
    bin_total = count_x * count_y * count_z
    flat_ids = neighbour_ids.reshape(bin_total, slot_count, atom_count)
    flat_counts = neighbour_counts.reshape(bin_total, atom_count)
    zero_index = jnp.zeros((), jnp.int32)

    def one_bin(bin_args):
        bin_index, bin_ids, bin_counts = bin_args
        cell_x = (bin_index // (count_y * count_z)).astype(jnp.int32)
        cell_y = (bin_index // count_z % count_y).astype(jnp.int32)
        cell_z = (bin_index % count_z).astype(jnp.int32)
        block_feat = lax.dynamic_slice(pad_feat, (cell_x, cell_y, cell_z, zero_index, zero_index), (3, 3, 3, atom_count, channel_count)).reshape(27 * atom_count, channel_count)
        block_pos = lax.dynamic_slice(pad_pos, (cell_x, cell_y, cell_z, zero_index, zero_index), (3, 3, 3, 3, atom_count))
        block_pos = jnp.moveaxis(block_pos, 3, 0).reshape(3, 27 * atom_count)
        return bin_energy(block_feat, block_pos, bin_ids, bin_counts, radial_weight, mix_weight, readout_weight, readout_vector, self_weight)
    energies = lax.map(jax.checkpoint(one_bin), (jnp.arange(bin_total, dtype=jnp.int32), flat_ids, flat_counts))
    return energies.reshape(count_x, count_y, count_z, atom_count)

def reference(features, positions, neighbour_ids, neighbour_counts, radial_weight, mix_weight, readout_weight, readout_vector, self_weight):
    widths = ((1, 1), (1, 1), (1, 1), (0, 0), (0, 0))
    pad_feat = jnp.pad(features, widths, mode='wrap')

    def grid_total(position_values):
        pad_pos = jnp.pad(position_values, widths, mode='wrap')
        return grid_energies(pad_feat, pad_pos, neighbour_ids, neighbour_counts, radial_weight, mix_weight, readout_weight, readout_vector, self_weight)
    atom_energy, pullback = jax.vjp(grid_total, positions.astype(jnp.float32))
    gradient = pullback(jnp.ones_like(atom_energy))[0]
    return (atom_energy, -gradient)
```

```python
import math

import jax
import jax.numpy as jnp
from jax import lax
from jax.experimental import pallas as pl
from jax.experimental.pallas import tpu as pltpu
from jax.sharding import PartitionSpec as P

C = 128; A = 128; K = 32; J = 8; H = 16
f32, bf16, i32, i16 = jnp.float32, jnp.bfloat16, jnp.int32, jnp.int16
R3, R5, R15 = math.sqrt(3.0), math.sqrt(5.0), math.sqrt(15.0)

def split(x):
    hi = x.astype(bf16)
    return hi, (x - hi.astype(f32)).astype(bf16)

def dot(a, b):
    return jnp.dot(a, b, preferred_element_type=f32)

def dot_nt(a, b):
    return lax.dot_general(a, b, (((1,), (1,)), ((), ())), preferred_element_type=f32)

def rows(x, n):
    return jnp.broadcast_to(x, (n, x.shape[1]))

def prepare_weights(rw_ref, mix_ref, ro_ref, rv_ref, sw_ref, rwt, mixt, mixn, rot, ron, rvc, sws):
    hi, lo = split(rw_ref[...])
    hi, lo = hi.astype(f32), lo.astype(f32)
    pad = jnp.zeros((96, 128), f32)
    for l in range(3):
        s = slice(l * 128, l * 128 + 128)
        x = jnp.concatenate([hi[:, s], hi[:, s], lo[:, s], lo[:, s], pad], axis=0)
        rwt[s, :] = x.T[:, :32].astype(bf16)
    for l in range(3):
        m = mix_ref[l]
        h, w = split(m.T)
        mixt[l, :, :] = jnp.concatenate([h, h, w], axis=1)
        h, w = split(m)
        mixn[l, :, :] = jnp.concatenate([h, h, w], axis=1)
    ro = ro_ref[...]
    h, w = split(ro)
    ron[...] = jnp.concatenate([h, h, w], axis=1)
    ropad = jnp.concatenate([ro, jnp.zeros((384, 112), f32)], axis=1)
    for l in range(3):
        h, w = split(ropad[l * 128:l * 128 + 128].T[:16])
        rot[l, :, :] = jnp.concatenate([h, h, w], axis=1)
    rvc[...] = jnp.broadcast_to(rv_ref[...], (128, 16)).T
    h, w = split(sw_ref[...])
    w2 = (sw_ref[...] - h.astype(f32) - w.astype(f32)).astype(bf16)
    ii = lax.broadcasted_iota(i32, (16, 128), 0)
    sws[...] = jnp.where(ii == 0, rows(h.astype(f32), 16), jnp.where(ii == 1, rows(w.astype(f32), 16), jnp.where(ii == 2, rows(w2.astype(f32), 16), 0.0))).astype(bf16)

def stack3(x):
    h, w = split(x)
    return jnp.concatenate([h, w, h], axis=0)

def geometry(ids_ref, cnt_ref, pos, rel, sq_ref, angb, radf):
    ids = ids_ref[...]
    q = ids >> 7
    slot = ids & 127
    acc = [jnp.zeros((K, A), f32) for _ in range(3)]
    for b in range(27):
        p = pos[HALO_OF[b]].astype(f32)
        m = q == b
        for c in range(3):
            t = jnp.take_along_axis(jnp.broadcast_to(p[c:c + 1], (K, A)), slot, axis=1)
            acc[c] = jnp.where(m, t, acc[c])
    q9 = (q * 57) >> 9
    q3 = (q * 43) >> 7
    off = [q9 - 1, q3 - 3 * q9 - 1, q - 3 * q3 - 1]
    own = pos[13].astype(f32)
    u, v, w = [(acc[c] + off[c].astype(f32)) - own[c:c + 1] for c in range(3)]
    sq = u * u + v * v + w * w
    rel[0] = u; rel[1] = v; rel[2] = w
    live = (lax.broadcasted_iota(i32, (K, A), 0) < cnt_ref[...]).astype(f32)
    e1 = 1.0 - sq / 16.0
    env = e1 * e1 * live
    denv = e1 * live * (-0.125)
    ang = [R3 * u, R3 * v, R3 * w, R15 * u * v, R15 * v * w, 0.5 * R5 * (3.0 * w * w - sq), R15 * u * w, 0.5 * R15 * (u * u - v * v)]
    decay = -0.08 * jnp.left_shift(1, lax.broadcasted_iota(i32, (J, A), 0)).astype(f32)
    for k in range(K):
        ks = slice(k, k + 1)
        for m in range(8):
            angb[m, k] = rows(ang[m][ks], 8)
        ex = jnp.exp(decay * rows(sq[ks], 8))
        r = ex * rows(env[ks], 8)
        dr = ex * (decay * rows(env[ks], 8) + rows(denv[ks], 8))
        for t, x in enumerate((r, dr)):
            hi = x.astype(bf16).astype(f32)
            y = jnp.concatenate([hi, x - hi], axis=0).astype(bf16)
            radf[k, t] = jnp.concatenate([y, y], axis=0)

def radial_maps(rwt, radf, S):
    w = rwt[...]
    def step(i, _):
        for t in range(2):
            x = jnp.concatenate([radf[2 * i, t], radf[2 * i + 1, t]], axis=1)
            y = dot(w, x)
            for l in range(3):
                for kk in range(2):
                    S[3 * t + l, 2 * i + kk] = y[l * 128:l * 128 + 128, kk * 128:kk * 128 + 128]
        return 0
    lax.fori_loop(0, K // 2, step, 0)

def amplitudes(G, S, angb, amp):
    def tile(ci, _):
        cs = pl.ds(pl.multiple_of(ci * 16, 16), 16)
        def step(k, acc):
            g = G[k, cs]
            h = []
            for l in range(3):
                x = g * S[l, k, cs]
                S[l, k, cs] = x
                h.append(x)
            out = [acc[0] + h[0]]
            for m in range(8):
                a = angb[m, k]
                a = jnp.concatenate([a, a], axis=0)
                out.append(acc[m + 1] + a * h[1 if m < 3 else 2])
            return tuple(out)
        acc = lax.fori_loop(0, K, step, tuple(jnp.zeros((16, A), f32) for _ in range(9)), unroll=4)
        for m in range(9):
            amp[m, cs] = acc[m]
        return 0
    lax.fori_loop(0, C // 16, tile, 0)

def readout(amp, mixt, mixn, rot, ron, rvc, sws, own, energy_ref):
    mixed = []
    for l, (lo, hi) in enumerate(((0, 1), (1, 4), (4, 9))):
        x = jnp.concatenate([amp[m] * 0.25 for m in range(lo, hi)], axis=1)
        y = dot(mixt[l], stack3(x))
        mixed += [y[:, 128 * i:128 * i + 128] for i in range(hi - lo)]
    inv = [mixed[0],
           mixed[1] * mixed[1] + mixed[2] * mixed[2] + mixed[3] * mixed[3],
           mixed[4] * mixed[4] + mixed[5] * mixed[5] + mixed[6] * mixed[6] + mixed[7] * mixed[7] + mixed[8] * mixed[8]]
    t = dot(rot[0], stack3(inv[0])) + dot(rot[1], stack3(inv[1])) + dot(rot[2], stack3(inv[2]))
    sg = 1.0 / (1.0 + jnp.exp(-t))
    self_e = dot(sws[...], own)
    energy_ref[...] = jnp.sum(rvc[...] * (t * sg), axis=0, keepdims=True) + jnp.sum(self_e, axis=0, keepdims=True)
    dh = rvc[...] * (sg * (1.0 + t * (1.0 - sg)))
    dinv = dot(ron[...], stack3(dh))
    d = [dinv[0:128], dinv[128:256] * 2.0, dinv[256:384] * 2.0]
    for l, (lo, hi) in enumerate(((0, 1), (1, 4), (4, 9))):
        x = jnp.concatenate([d[l] if l == 0 else d[l] * mixed[m] for m in range(lo, hi)], axis=1)
        y = dot(mixn[l], stack3(x)) * 0.25
        for i in range(hi - lo):
            amp[lo + i] = y[:, 128 * i:128 * i + 128]

def edge_gradients(G, S, angb, damp, dA):
    def step(k, _):
        a = [angb[m, k] for m in range(8)]
        acc = [jnp.zeros((8, A), f32) for _ in range(9)]
        for ci in range(16):
            cs = slice(8 * ci, 8 * ci + 8)
            h1, h2 = S[1, k, cs], S[2, k, cs]
            dm = [damp[m, cs] for m in range(9)]
            for m in range(8):
                acc[m + 1] = acc[m + 1] + (h1 if m < 3 else h2) * dm[m + 1]
            t1 = a[0] * dm[1] + a[1] * dm[2] + a[2] * dm[3]
            t2 = (a[3] * dm[4] + a[4] * dm[5]) + (a[5] * dm[6] + a[6] * dm[7]) + a[7] * dm[8]
            acc[0] = acc[0] + G[k, cs] * (S[3, k, cs] * dm[0] + S[4, k, cs] * t1 + S[5, k, cs] * t2)
        for m in range(9):
            dA[m, pl.ds(k, 1)] = jnp.sum(acc[m], axis=0, keepdims=True)
        return 0
    lax.fori_loop(0, K, step, 0)

def forces_out(ids_ref, rel, dA, D):
    u, v, w = rel[0], rel[1], rel[2]
    dS, d1, d2, d3, d4, d5, d6, d7, d8 = [dA[m] for m in range(9)]
    base = 2.0 * dS - R5 * d6
    gu = base * u + R3 * d1 + R15 * (v * d4 + w * d7 + u * d8)
    gv = base * v + R3 * d2 + R15 * (u * d4 + w * d5 - v * d8)
    gw = 2.0 * w * (dS + R5 * d6) + R3 * d3 + R15 * (v * d5 + u * d7)
    g = [gu, gv, gw]
    parts = []
    for x in g:
        hi = x.astype(bf16).astype(f32)
        parts += [hi, x - hi]
    ii = lax.broadcasted_iota(i32, (8, A), 0)
    iot = lax.broadcasted_iota(i32, (16, A), 0)
    acc = None
    ids = ids_ref[...]
    for c in range(0, K, 2):
        lhs, rhs = [], []
        for k in (c, c + 1):
            x = jnp.zeros((8, A), f32)
            for j, (p, r) in enumerate(((0, 0), (2, 1), (4, 2), (1, 4), (3, 5), (5, 6))):
                x = jnp.where(ii == r, rows(parts[p][k:k + 1], 8), x)
            idr = rows(ids[k:k + 1], 8)
            qk = idr >> 7
            col = [jnp.where(qk == b, x, 0.0) for b in range(27)] + [jnp.zeros((8, A), f32)]
            lhs.append(jnp.concatenate(col, axis=0).astype(bf16))
            s = rows(ids[k:k + 1], 16) & 127
            rhs.append(jnp.concatenate([jnp.where(s == iot + 16 * r, 1.0, 0.0).astype(bf16) for r in range(8)], axis=0))
        y = dot_nt(jnp.concatenate(lhs, axis=1), jnp.concatenate(rhs, axis=1))
        acc = y if acc is None else acc + y
    for b in range(27):
        y = acc[8 * b:8 * b + 8]
        D[HALO_OF[b]] = y[0:4] + y[4:8] if b != 13 else y[0:4] + y[4:8] - jnp.concatenate([jnp.sum(x, axis=0, keepdims=True) for x in g] + [jnp.zeros((1, A), f32)], axis=0)

MESH = pl.DeviceIdType.MESH
def bin_of(h):
    return (h // 3 % 3) * 9 + (h % 3) * 3 + h // 9


HALO_OF = {bin_of(h): h for h in range(27)}


def gather(ids_ref, feat, G, blocks, first):
    iot = lax.broadcasted_iota(i32, (16, A), 0)

    def step(i, _):
        slots, qs = [], []
        for kk in range(2):
            row = jnp.broadcast_to(ids_ref[pl.ds(2 * i + kk, 1), :], (16, A))
            qs.append((row >> 7).astype(i16))
            s = row & 127
            slots.append([jnp.where(s == iot + 16 * r, 1.0, 0.0).astype(bf16) for r in range(8)])
        z = jnp.zeros((16, A), bf16)
        acc = None
        for t in range(0, len(blocks), 2):
            pair = blocks[t:t + 2]
            cols = []
            for kk in range(2):
                pieces = []
                for h in pair:
                    m = qs[kk] == jnp.int16(bin_of(h))
                    pieces += [jnp.where(m, slots[kk][r], z) for r in range(8)]
                cols.append(jnp.concatenate(pieces, axis=0))
            e = jnp.concatenate(cols, axis=1)
            f = jnp.concatenate([feat[h] for h in pair], axis=1)
            y = dot(f, e)
            acc = y if acc is None else acc + y
        for kk in range(2):
            y = acc[:, kk * 128:kk * 128 + 128]
            G[2 * i + kk] = y if first else G[2 * i + kk] + y
        return 0

    lax.fori_loop(0, K // 2, step, 0)


def kernel(sizes, f_ref, p_ref, ids_ref, cnt_ref, rw_ref, mix_ref, ro_ref, rv_ref, sw_ref, en_ref, out_ref,
           feat, hpos, rwt, mixt, mixn, rot, ron, rvc, sws, rel, sqr, angb, radf, S, G, amp, dA,
           D, back_z, back_x, back_y, fs, fr, ps, pr, bs, br):
    near = {}
    for axis in ("gx", "gy", "gz"):
        me = lax.axis_index(axis)
        near[axis, 1] = {axis: lax.rem(me + 1, sizes[axis])}
        near[axis, -1] = {axis: lax.rem(me + sizes[axis] - 1, sizes[axis])}

    def remote(src, dst, send, recv, axis, way):
        return pltpu.make_async_remote_copy(src_ref=src, dst_ref=dst, send_sem=send, recv_sem=recv,
                                            device_id=near[axis, way], device_id_type=MESH)

    barrier = pltpu.get_barrier_semaphore()
    for target in near.values():
        pl.semaphore_signal(barrier, inc=1, device_id=target, device_id_type=MESH)
    feat[13] = f_ref[...].astype(f32).T.astype(bf16)
    hpos[13] = jnp.concatenate([p_ref[...].astype(f32), jnp.zeros((13, A), f32)], axis=0).astype(bf16)
    pl.semaphore_wait(barrier, 6)

    pos = {}
    for n, (axis, way, src, dst) in enumerate((
            ("gy", 1, (13, 1), (12, 1)), ("gy", -1, (13, 1), (14, 1)),
            ("gx", 1, (12, 3), (9, 3)), ("gx", -1, (12, 3), (15, 3)),
            ("gz", 1, (9, 9), (0, 9)), ("gz", -1, (9, 9), (18, 9)))):
        pos[axis, way] = remote(hpos.at[pl.ds(*src)], hpos.at[pl.ds(*dst)], ps.at[n], pr.at[n], axis, way)
    moves = {}

    def move(src, dst, axis, way):
        moves[dst] = remote(feat.at[src], feat.at[dst], fs.at[dst], fr.at[dst], axis, way)

    move(13, 12, "gy", 1)
    move(13, 14, "gy", -1)
    for y in range(3):
        move(12 + y, 9 + y, "gx", 1)
        move(12 + y, 15 + y, "gx", -1)
    for xy in range(9):
        move(9 + xy, xy, "gz", 1)
        move(9 + xy, 18 + xy, "gz", -1)

    def start(*blocks):
        for h in blocks:
            moves[h].start()

    def arrive(*blocks):
        for h in blocks:
            moves[h].wait_recv()

    def both(axis, what):
        for way in (1, -1):
            getattr(pos[axis, way], what)()

    both("gy", "start")
    start(12, 14, 10, 16, 4, 22)
    prepare_weights(rw_ref, mix_ref, ro_ref, rv_ref, sw_ref, rwt, mixt, mixn, rot, ron, rvc, sws)
    both("gy", "wait_recv")
    both("gx", "start")
    arrive(12, 14)
    start(9, 15, 11, 17, 3, 21, 5, 23)
    both("gx", "wait_recv")
    both("gz", "start")
    arrive(10, 16)
    start(1, 19, 7, 25)
    arrive(9, 15, 11, 17)
    start(0, 18, 6, 24, 2, 20, 8, 26)
    both("gz", "wait_recv")
    geometry(ids_ref, cnt_ref, hpos, rel, sqr, angb, radf)
    radial_maps(rwt, radf, S)
    gather(ids_ref, feat, G, tuple(range(9, 18)), True)
    arrive(*range(9))
    gather(ids_ref, feat, G, tuple(range(9)), False)
    arrive(*range(18, 27))
    gather(ids_ref, feat, G, tuple(range(18, 27)), False)
    amplitudes(G, S, angb, amp)
    readout(amp, mixt, mixn, rot, ron, rvc, sws, feat[13], en_ref)
    edge_gradients(G, S, angb, amp, dA)
    forces_out(ids_ref, rel, dA, D)

    def exchange(n, src_low, src_high, landing, axis):
        low = remote(src_low, landing.at[0], bs.at[n], br.at[n], axis, -1)
        high = remote(src_high, landing.at[1], bs.at[n + 1], br.at[n + 1], axis, 1)
        low.start()
        high.start()
        low.wait()
        high.wait()

    exchange(0, D.at[pl.ds(0, 9)], D.at[pl.ds(18, 9)], back_z, "gz")
    D[9:18] = D[9:18] + back_z[0] + back_z[1]
    exchange(2, D.at[pl.ds(9, 3)], D.at[pl.ds(15, 3)], back_x, "gx")
    D[12:15] = D[12:15] + back_x[0] + back_x[1]
    exchange(4, D.at[12], D.at[14], back_y, "gy")
    out_ref[...] = -(D[13] + back_y[0] + back_y[1])[0:3]
    for copy in list(moves.values()) + list(pos.values()):
        copy.wait_send()


def solution(mesh):
    sizes = dict(mesh.shape)
    V, DMA = pltpu.VMEM, pltpu.SemaphoreType.DMA

    def body(features, positions, ids, counts, rw, mix, ro, rv, sw):
        energy, forces = pl.pallas_call(
            lambda *refs: kernel(sizes, *refs),
            out_shape=(jax.ShapeDtypeStruct((1, A), f32), jax.ShapeDtypeStruct((3, A), f32)),
            scratch_shapes=[
                V((27, C, A), bf16), V((27, 16, A), bf16), V((384, 32), bf16), V((3, C, 384), bf16), V((3, C, 384), bf16),
                V((3, H, 384), bf16), V((384, 48), bf16), V((H, A), f32), V((16, C), bf16), V((3, K, A), f32), V((K, A), f32),
                V((8, K, 8, A), f32), V((K, 2, 32, A), bf16), V((6, K, C, A), f32), V((K, C, A), f32), V((9, C, A), f32),
                V((9, K, A), f32), V((27, 4, A), f32), V((2, 9, 4, A), f32), V((2, 3, 4, A), f32), V((2, 4, A), f32),
                DMA((27,)), DMA((27,)), DMA((6,)), DMA((6,)), DMA((6,)), DMA((6,)),
            ],
            compiler_params=pltpu.CompilerParams(collective_id=0, has_side_effects=True, vmem_limit_bytes=48 * 2**20),
        )(features.reshape(A, C), positions.reshape(3, A), ids.reshape(K, A), counts.reshape(1, A), rw, mix, ro,
          rv.reshape(1, H), sw.reshape(1, C))
        return energy.reshape(1, 1, 1, A), forces.reshape(1, 1, 1, 3, A)

    block = ("gx", "gy", "gz")
    in_specs = (P(*block, None, None),) * 3 + (P(*block, None),) + (P(),) * 5
    out_specs = (P(*block, None), P(*block, None, None))
    return jax.shard_map(body, mesh=mesh, in_specs=in_specs, out_specs=out_specs, check_vma=False)
```

```python
import functools, math
HALO_OF = {b: b for b in range(27)}
import jax, jax.numpy as jnp
from jax import lax
from jax.experimental import pallas as pl
from jax.experimental.pallas import tpu as pltpu
from jax.sharding import PartitionSpec as P

C = 128; A = 128; K = 32; J = 8; H = 16
f32, bf16, i32, i16 = jnp.float32, jnp.bfloat16, jnp.int32, jnp.int16
R3, R5, R15 = math.sqrt(3.0), math.sqrt(5.0), math.sqrt(15.0)

def split(x):
    hi = x.astype(bf16)
    return hi, (x - hi.astype(f32)).astype(bf16)

def dot(a, b):
    return jnp.dot(a, b, preferred_element_type=f32)

def dot_nt(a, b):
    return lax.dot_general(a, b, (((1,), (1,)), ((), ())), preferred_element_type=f32)

def rows(x, n):
    return jnp.broadcast_to(x, (n, x.shape[1]))

def prepare_weights(rw_ref, mix_ref, ro_ref, rv_ref, sw_ref, rwt, mixt, mixn, rot, ron, rvc, sws):
    hi, lo = split(rw_ref[...])
    hi, lo = hi.astype(f32), lo.astype(f32)
    pad = jnp.zeros((96, 128), f32)
    for l in range(3):
        s = slice(l * 128, l * 128 + 128)
        x = jnp.concatenate([hi[:, s], hi[:, s], lo[:, s], lo[:, s], pad], axis=0)
        rwt[s, :] = x.T[:, :32].astype(bf16)
    for l in range(3):
        m = mix_ref[l]
        h, w = split(m.T)
        mixt[l, :, :] = jnp.concatenate([h, h, w], axis=1)
        h, w = split(m)
        mixn[l, :, :] = jnp.concatenate([h, h, w], axis=1)
    for l in range(3):
        s = slice(l * 128, l * 128 + 128)
        x = ro_ref[:, s]
        h, w = split(x)
        rot[l, :, :] = jnp.concatenate([h, h, w], axis=1)
        h, w = split(jnp.concatenate([x, jnp.zeros((112, 128), f32)], axis=0).T[:, :16])
        ron[s, :] = jnp.concatenate([h, h, w], axis=1)
    rvc[...] = jnp.broadcast_to(rv_ref[...], (128, 16)).T
    h, w = split(sw_ref[...])
    w2 = (sw_ref[...] - h.astype(f32) - w.astype(f32)).astype(bf16)
    ii = lax.broadcasted_iota(i32, (16, 128), 0)
    sws[...] = jnp.where(ii == 0, rows(h.astype(f32), 16), jnp.where(ii == 1, rows(w.astype(f32), 16), jnp.where(ii == 2, rows(w2.astype(f32), 16), 0.0))).astype(bf16)

def stack3(x):
    h, w = split(x)
    return jnp.concatenate([h, w, h], axis=0)

def geometry(ids_ref, cnt_ref, pos, rel, sq_ref, angb, radf):
    ids = ids_ref[...]
    q = ids >> 7
    slot = ids & 127
    acc = [jnp.zeros((K, A), f32) for _ in range(3)]
    for b in range(27):
        p = pos[HALO_OF[b]].astype(f32)
        m = q == b
        for c in range(3):
            t = jnp.take_along_axis(jnp.broadcast_to(p[c:c + 1], (K, A)), slot, axis=1)
            acc[c] = jnp.where(m, t, acc[c])
    q9 = (q * 57) >> 9
    q3 = (q * 43) >> 7
    off = [q9 - 1, q3 - 3 * q9 - 1, q - 3 * q3 - 1]
    own = pos[13].astype(f32)
    u, v, w = [(acc[c] + off[c].astype(f32)) - own[c:c + 1] for c in range(3)]
    sq = u * u + v * v + w * w
    rel[0] = u; rel[1] = v; rel[2] = w
    live = (lax.broadcasted_iota(i32, (K, A), 0) < cnt_ref[...]).astype(f32)
    e1 = 1.0 - sq / 16.0
    env = e1 * e1 * live
    denv = e1 * live * (-0.125)
    ang = [R3 * u, R3 * v, R3 * w, R15 * u * v, R15 * v * w, 0.5 * R5 * (3.0 * w * w - sq), R15 * u * w, 0.5 * R15 * (u * u - v * v)]
    decay = -0.08 * jnp.left_shift(1, lax.broadcasted_iota(i32, (J, A), 0)).astype(f32)
    for k in range(K):
        ks = slice(k, k + 1)
        for m in range(8):
            angb[m, k] = rows(ang[m][ks], 8)
        ex = jnp.exp(decay * rows(sq[ks], 8))
        r = ex * rows(env[ks], 8)
        dr = ex * (decay * rows(env[ks], 8) + rows(denv[ks], 8))
        for t, x in enumerate((r, dr)):
            hi = x.astype(bf16).astype(f32)
            y = jnp.concatenate([hi, x - hi], axis=0).astype(bf16)
            radf[k, t] = jnp.concatenate([y, y], axis=0)

def radial_maps(rwt, radf, S, lo, hi, n=8):
    w = rwt[...]

    def step(i, _):
        x = jnp.concatenate([radf[n * i + kk, t] for t in range(2) for kk in range(n)], axis=1)
        y = dot(w, x)
        for t in range(2):
            for l in range(3):
                for kk in range(n):
                    c = (t * n + kk) * 128
                    S[3 * t + l, n * i + kk] = y[l * 128:l * 128 + 128, c:c + 128]
        return 0

    lax.fori_loop(lo // n, hi // n, step, 0)


def amplitudes(G, S, angb, amp):
    def tile(ci, _):
        cs = pl.ds(pl.multiple_of(ci * 16, 16), 16)
        def step(k, acc):
            g = G[k, cs]
            h = []
            for l in range(3):
                x = g * S[l, k, cs]
                S[l, k, cs] = x
                h.append(x)
            out = [acc[0] + h[0]]
            for m in range(8):
                a = angb[m, k]
                a = jnp.concatenate([a, a], axis=0)
                out.append(acc[m + 1] + a * h[1 if m < 3 else 2])
            return tuple(out)
        acc = lax.fori_loop(0, K, step, tuple(jnp.zeros((16, A), f32) for _ in range(9)), unroll=8)
        for m in range(9):
            amp[m, cs] = acc[m]
        return 0
    lax.fori_loop(0, C // 16, tile, 0)

def readout(amp, mixt, mixn, rot, ron, rvc, sws, own, energy_ref):
    mixed = []
    for l, (lo, hi) in enumerate(((0, 1), (1, 4), (4, 9))):
        x = jnp.concatenate([amp[m] * 0.25 for m in range(lo, hi)], axis=1)
        y = dot(mixt[l], stack3(x))
        mixed += [y[:, 128 * i:128 * i + 128] for i in range(hi - lo)]
    inv = [mixed[0],
           mixed[1] * mixed[1] + mixed[2] * mixed[2] + mixed[3] * mixed[3],
           mixed[4] * mixed[4] + mixed[5] * mixed[5] + mixed[6] * mixed[6] + mixed[7] * mixed[7] + mixed[8] * mixed[8]]
    t = dot(rot[0], stack3(inv[0])) + dot(rot[1], stack3(inv[1])) + dot(rot[2], stack3(inv[2]))
    sg = 1.0 / (1.0 + jnp.exp(-t))
    self_e = dot(sws[...], own)
    energy_ref[...] = jnp.sum(rvc[...] * (t * sg), axis=0, keepdims=True) + jnp.sum(self_e, axis=0, keepdims=True)
    dh = rvc[...] * (sg * (1.0 + t * (1.0 - sg)))
    dinv = dot(ron[...], stack3(dh))
    d = [dinv[0:128], dinv[128:256] * 2.0, dinv[256:384] * 2.0]
    for l, (lo, hi) in enumerate(((0, 1), (1, 4), (4, 9))):
        x = jnp.concatenate([d[l] if l == 0 else d[l] * mixed[m] for m in range(lo, hi)], axis=1)
        y = dot(mixn[l], stack3(x)) * 0.25
        for i in range(hi - lo):
            amp[lo + i] = y[:, 128 * i:128 * i + 128]

def edge_gradients(G, S, angb, damp, dA):
    def step(k, _):
        a = [angb[m, k] for m in range(8)]
        acc = [jnp.zeros((8, A), f32) for _ in range(9)]
        for ci in range(16):
            cs = slice(8 * ci, 8 * ci + 8)
            h1, h2 = S[1, k, cs], S[2, k, cs]
            dm = [damp[m, cs] for m in range(9)]
            for m in range(8):
                acc[m + 1] = acc[m + 1] + (h1 if m < 3 else h2) * dm[m + 1]
            t1 = a[0] * dm[1] + a[1] * dm[2] + a[2] * dm[3]
            t2 = (a[3] * dm[4] + a[4] * dm[5]) + (a[5] * dm[6] + a[6] * dm[7]) + a[7] * dm[8]
            acc[0] = acc[0] + G[k, cs] * (S[3, k, cs] * dm[0] + S[4, k, cs] * t1 + S[5, k, cs] * t2)
        for m in range(9):
            dA[m, pl.ds(k, 1)] = jnp.sum(acc[m], axis=0, keepdims=True)
        return 0
    lax.fori_loop(0, K, step, 0)

def forces_out(ids_ref, rel, dA, D):
    u, v, w = rel[0], rel[1], rel[2]
    dS, d1, d2, d3, d4, d5, d6, d7, d8 = [dA[m] for m in range(9)]
    base = 2.0 * dS - R5 * d6
    gu = base * u + R3 * d1 + R15 * (v * d4 + w * d7 + u * d8)
    gv = base * v + R3 * d2 + R15 * (u * d4 + w * d5 - v * d8)
    gw = 2.0 * w * (dS + R5 * d6) + R3 * d3 + R15 * (v * d5 + u * d7)
    g = [gu, gv, gw]
    parts = []
    for x in g:
        hi = x.astype(bf16).astype(f32)
        parts += [hi, x - hi]
    ii = lax.broadcasted_iota(i32, (8, A), 0)
    iot = lax.broadcasted_iota(i32, (16, A), 0)
    acc = None
    ids = ids_ref[...]
    for c in range(0, K, 2):
        lhs, rhs = [], []
        for k in (c, c + 1):
            x = jnp.zeros((8, A), f32)
            for j, (p, r) in enumerate(((0, 0), (2, 1), (4, 2), (1, 4), (3, 5), (5, 6))):
                x = jnp.where(ii == r, rows(parts[p][k:k + 1], 8), x)
            idr = rows(ids[k:k + 1], 8)
            qk = idr >> 7
            col = [jnp.where(qk == b, x, 0.0) for b in range(27)] + [jnp.zeros((8, A), f32)]
            lhs.append(jnp.concatenate(col, axis=0).astype(bf16))
            s = rows(ids[k:k + 1], 16) & 127
            rhs.append(jnp.concatenate([jnp.where(s == iot + 16 * r, 1.0, 0.0).astype(bf16) for r in range(8)], axis=0))
        y = dot_nt(jnp.concatenate(lhs, axis=1), jnp.concatenate(rhs, axis=1))
        acc = y if acc is None else acc + y
    for b in range(27):
        y = acc[8 * b:8 * b + 8]
        D[SLOT_OF[b]] = y[0:4] + y[4:8] if b != 13 else y[0:4] + y[4:8] - jnp.concatenate([jnp.sum(x, axis=0, keepdims=True) for x in g] + [jnp.zeros((1, A), f32)], axis=0)

MESH = pl.DeviceIdType.MESH
def bin_of(h):
    return (h // 3 % 3) * 9 + (h % 3) * 3 + h // 9


HALO_OF = {bin_of(h): h for h in range(27)}
AROUND = tuple(h for h in range(27) if h != 13)
SLOT = {h: i for i, h in enumerate(AROUND + (13,))}
SLOT_OF = {bin_of(h): i for h, i in SLOT.items()}


def gather(ids_ref, feat, G, blocks, first, n=4):
    iot = lax.broadcasted_iota(i32, (16, A), 0)

    def step(i, _):
        slots, qs = [], []
        for kk in range(n):
            row = jnp.broadcast_to(ids_ref[pl.ds(n * i + kk, 1), :], (16, A))
            qs.append((row >> 7).astype(i16))
            s = row & 127
            slots.append([jnp.where(s == iot + 16 * r, 1.0, 0.0).astype(bf16) for r in range(8)])
        z = jnp.zeros((16, A), bf16)
        acc = None
        for t in range(0, len(blocks), 2):
            pair = blocks[t:t + 2]
            cols = []
            for kk in range(n):
                pieces = []
                for h in pair:
                    m = qs[kk] == jnp.int16(bin_of(h))
                    pieces += [jnp.where(m, slots[kk][r], z) for r in range(8)]
                cols.append(jnp.concatenate(pieces, axis=0))
            e = jnp.concatenate(cols, axis=1)
            f = jnp.concatenate([feat[h] for h in pair], axis=1)
            y = dot(f, e)
            acc = y if acc is None else acc + y
        for kk in range(n):
            y = acc[:, kk * 128:kk * 128 + 128]
            G[n * i + kk] = y if first else G[n * i + kk] + y
        return 0

    lax.fori_loop(0, K // n, step, 0)


def kernel(sizes, f_hbm, p_hbm, ids_hbm, cnt_hbm, rw_hbm, mix_hbm, ro_hbm, rv_hbm, sw_hbm, en_ref, out_ref,
           f_ref, p_ref, ids_ref, cnt_ref, rw_ref, mix_ref, ro_ref, rv_ref, sw_ref,
           feat, hpos, rwt, mixt, mixn, rot, ron, rvc, sws, rel, sqr, angb, radf, S, G, amp, dA,
           D, landing, ls, fs, fr, ps, pr, bs, br):
    place = {}
    for axis in sizes:
        me, size = lax.axis_index(axis), sizes[axis]
        place[axis] = (jnp.where(me == 0, size - 1, me - 1), me, jnp.where(me == size - 1, 0, me + 1))

    def device(h):
        return {"gx": place["gx"][h // 3 % 3], "gy": place["gy"][h % 3], "gz": place["gz"][h // 9]}

    def remote(h, src, dst, send, recv):
        return pltpu.make_async_remote_copy(src_ref=src, dst_ref=dst, send_sem=send, recv_sem=recv,
                                            device_id=device(h), device_id_type=MESH)

    plane = (10, 16, 12, 14, 9, 11, 15, 17)
    barrier = pltpu.get_barrier_semaphore()
    for h in (4, 22) + plane:
        pl.semaphore_signal(barrier, inc=1, device_id=device(h), device_id_type=MESH)
    local = [pltpu.make_async_copy(src, dst, ls.at[i]) for i, (src, dst) in enumerate((
        (f_hbm, f_ref), (p_hbm, p_ref), (rw_hbm, rw_ref), (mix_hbm, mix_ref), (ro_hbm, ro_ref), (rv_hbm, rv_ref),
        (sw_hbm, sw_ref), (ids_hbm, ids_ref), (cnt_hbm, cnt_ref)))]
    for copy in local:
        copy.start()
    local[0].wait()
    local[1].wait()
    feat[13] = f_ref[...].astype(f32).T.astype(bf16)
    hpos[13] = jnp.concatenate([p_ref[...].astype(f32), jnp.zeros((13, A), f32)], axis=0).astype(bf16)
    pl.semaphore_wait(barrier, 10)

    pos = [remote(h, hpos.at[13], hpos.at[26 - h], ps.at[i], pr.at[i]) for i, h in enumerate(plane)]
    pos_z = [remote(h, hpos.at[pl.ds(9, 9)], hpos.at[pl.ds(18 - h // 9 * 9, 9)], ps.at[8 + i], pr.at[8 + i])
             for i, h in enumerate((4, 22))]
    feat_y = [remote(h, feat.at[13], feat.at[26 - h], fs.at[i], fr.at[i]) for i, h in enumerate((12, 14))]
    feat_x = [remote(h, feat.at[pl.ds(12, 3)], feat.at[pl.ds(24 - (h - 1), 3)], fs.at[2 + i], fr.at[2 + i])
              for i, h in enumerate((10, 16))]
    feat_z = [[remote(h, feat.at[pl.ds(9 + 3 * x, 3)], feat.at[pl.ds(18 - h // 9 * 9 + 3 * x, 3)],
                      fs.at[4 + 2 * x + i], fr.at[4 + 2 * x + i]) for i, h in enumerate((4, 22))] for x in range(3)]

    def start(copies):
        for copy in copies:
            copy.start()

    def arrive(copies):
        for copy in copies:
            copy.wait_recv()

    start(pos)
    start(feat_y)
    for copy in local[2:]:
        copy.wait()
    prepare_weights(rw_ref, mix_ref, ro_ref, rv_ref, sw_ref, rwt, mixt, mixn, rot, ron, rvc, sws)
    arrive(pos)
    start(pos_z)
    arrive(feat_y)
    start(feat_x)
    start(feat_z[1])
    arrive(pos_z)
    geometry(ids_ref, cnt_ref, hpos, rel, sqr, angb, radf)
    radial_maps(rwt, radf, S, 0, 8)
    arrive(feat_x)
    start(feat_z[0])
    start(feat_z[2])
    radial_maps(rwt, radf, S, 8, K)
    gather(ids_ref, feat, G, tuple(range(9, 18)), True)
    arrive(feat_z[1])
    gather(ids_ref, feat, G, (3, 4, 5, 21, 22, 23), False)
    arrive(feat_z[0])
    arrive(feat_z[2])
    gather(ids_ref, feat, G, (0, 1, 2, 6, 7, 8, 18, 19, 20, 24, 25, 26), False)
    amplitudes(G, S, angb, amp)
    readout(amp, mixt, mixn, rot, ron, rvc, sws, feat[13], en_ref)
    edge_gradients(G, S, angb, amp, dA)
    forces_out(ids_ref, rel, dA, D)

    start([remote(h, D.at[SLOT[h]], landing.at[SLOT[26 - h]], bs.at[0], br.at[0]) for h in AROUND])
    for copy in pos + pos_z + feat_y + feat_x + feat_z[0] + feat_z[1] + feat_z[2]:
        copy.wait_send()
    every = pl.ds(0, 26)
    pltpu.make_async_copy(landing.at[every], landing.at[every], br.at[0]).wait()
    total = D[26]
    for i in range(26):
        total = total + landing[i]
    out_ref[...] = -total[0:3]
    pltpu.make_async_copy(D.at[every], D.at[every], bs.at[0]).wait()


def solution(mesh):
    sizes = dict(mesh.shape)
    V, DMA = pltpu.VMEM, pltpu.SemaphoreType.DMA

    def body(features, positions, ids, counts, rw, mix, ro, rv, sw):
        energy, forces = pl.pallas_call(
            lambda *refs: kernel(sizes, *refs),
            out_shape=(jax.ShapeDtypeStruct((1, A), f32), jax.ShapeDtypeStruct((3, A), f32)),
            in_specs=[pl.BlockSpec(memory_space=pltpu.HBM)] * 9,
            scratch_shapes=[
                V((A, C), bf16), V((3, A), bf16), V((K, A), i32), V((1, A), i32), V((J, 384), f32), V((3, C, C), f32),
                V((H, 384), f32), V((1, H), f32), V((1, C), f32),
                V((27, C, A), bf16), V((27, 16, A), bf16), V((384, 32), bf16), V((3, C, 384), bf16), V((3, C, 384), bf16),
                V((3, H, 384), bf16), V((384, 48), bf16), V((H, A), f32), V((16, C), bf16), V((3, K, A), f32), V((K, A), f32),
                V((8, K, 8, A), f32), V((K, 2, 32, A), bf16), V((6, K, C, A), f32), V((K, C, A), f32), V((9, C, A), f32),
                V((9, K, A), f32), V((27, 4, A), f32), V((26, 4, A), f32),
                DMA((9,)), DMA((10,)), DMA((10,)), DMA((10,)), DMA((10,)), DMA((1,)), DMA((1,)),
            ],
            compiler_params=pltpu.CompilerParams(collective_id=0, has_side_effects=True, vmem_limit_bytes=48 * 2**20),
        )(*(pltpu.with_memory_space_constraint(x, pltpu.HBM) for x in (
            features.reshape(A, C), positions.reshape(3, A), ids.reshape(K, A), counts.reshape(1, A), rw, mix, ro.T,
            rv.reshape(1, H), sw.reshape(1, C))))
        return energy.reshape(1, 1, 1, A), forces.reshape(1, 1, 1, 3, A)

    block = ("gx", "gy", "gz")
    in_specs = (P(*block, None, None),) * 3 + (P(*block, None),) + (P(),) * 5
    out_specs = (P(*block, None), P(*block, None, None))
    return jax.shard_map(body, mesh=mesh, in_specs=in_specs, out_specs=out_specs, check_vma=False)
```

```python
import functools, math
HALO_OF = {b: b for b in range(27)}
import jax, jax.numpy as jnp
from jax import lax
from jax.experimental import pallas as pl
from jax.experimental.pallas import tpu as pltpu
from jax.sharding import PartitionSpec as P

C = 128; A = 128; K = 32; J = 8; H = 16
f32, bf16, i32, i16 = jnp.float32, jnp.bfloat16, jnp.int32, jnp.int16
R3, R5, R15 = math.sqrt(3.0), math.sqrt(5.0), math.sqrt(15.0)

def split(x):
    hi = x.astype(bf16)
    return hi, (x - hi.astype(f32)).astype(bf16)

def dot(a, b):
    return jnp.dot(a, b, preferred_element_type=f32)

def dot_nt(a, b):
    return lax.dot_general(a, b, (((1,), (1,)), ((), ())), preferred_element_type=f32)

def rows(x, n):
    return jnp.broadcast_to(x, (n, x.shape[1]))

def prepare_weights(rw_ref, mix_ref, ro_ref, rv_ref, sw_ref, rwt, mixt, mixn, rot, ron, rvc, sws):
    hi, lo = split(rw_ref[...])
    hi, lo = hi.astype(f32), lo.astype(f32)
    pad = jnp.zeros((96, 128), f32)
    for l in range(3):
        s = slice(l * 128, l * 128 + 128)
        x = jnp.concatenate([hi[:, s], hi[:, s], lo[:, s], lo[:, s], pad], axis=0)
        rwt[s, :] = x.T[:, :32].astype(bf16)
    for l in range(3):
        m = mix_ref[l]
        h, w = split(m.T)
        mixt[l, :, :] = jnp.concatenate([h, h, w], axis=1)
        h, w = split(m)
        mixn[l, :, :] = jnp.concatenate([h, h, w], axis=1)
    for l in range(3):
        s = slice(l * 128, l * 128 + 128)
        x = ro_ref[:, s]
        h, w = split(x)
        rot[l, :, :] = jnp.concatenate([h, h, w], axis=1)
        h, w = split(jnp.concatenate([x, jnp.zeros((112, 128), f32)], axis=0).T[:, :16])
        ron[s, :] = jnp.concatenate([h, h, w], axis=1)
    rvc[...] = jnp.broadcast_to(rv_ref[...], (128, 16)).T
    h, w = split(sw_ref[...])
    w2 = (sw_ref[...] - h.astype(f32) - w.astype(f32)).astype(bf16)
    ii = lax.broadcasted_iota(i32, (16, 128), 0)
    sws[...] = jnp.where(ii == 0, rows(h.astype(f32), 16), jnp.where(ii == 1, rows(w.astype(f32), 16), jnp.where(ii == 2, rows(w2.astype(f32), 16), 0.0))).astype(bf16)

def stack3(x):
    h, w = split(x)
    return jnp.concatenate([h, w, h], axis=0)

def geometry(ids_ref, cnt_ref, pos, rel, angb, radf):
    ids = ids_ref[...]
    q = ids >> 7
    slot = ids & 127
    acc = [jnp.zeros((K, A), f32) for _ in range(3)]
    for b in range(27):
        p = pos[HALO_OF[b]].astype(f32)
        m = q == b
        for c in range(3):
            t = jnp.take_along_axis(jnp.broadcast_to(p[c:c + 1], (K, A)), slot, axis=1)
            acc[c] = jnp.where(m, t, acc[c])
    q9 = (q * 57) >> 9
    q3 = (q * 43) >> 7
    off = [q9 - 1, q3 - 3 * q9 - 1, q - 3 * q3 - 1]
    own = pos[13].astype(f32)
    u, v, w = [(acc[c] + off[c].astype(f32)) - own[c:c + 1] for c in range(3)]
    sq = u * u + v * v + w * w
    rel[0] = u; rel[1] = v; rel[2] = w
    live = (lax.broadcasted_iota(i32, (K, A), 0) < cnt_ref[...]).astype(f32)
    e1 = 1.0 - sq / 16.0
    env = e1 * e1 * live
    denv = e1 * live * (-0.125)
    ang = [R3 * u, R3 * v, R3 * w, R15 * u * v, R15 * v * w, 0.5 * R5 * (3.0 * w * w - sq), R15 * u * w, 0.5 * R15 * (u * u - v * v)]
    decay = -0.08 * jnp.left_shift(1, lax.broadcasted_iota(i32, (J, A), 0)).astype(f32)
    for k in range(K):
        ks = slice(k, k + 1)
        for m in range(8):
            angb[m, k] = rows(ang[m][ks], 8)
        ex = jnp.exp(decay * rows(sq[ks], 8))
        r = ex * rows(env[ks], 8)
        dr = ex * (decay * rows(env[ks], 8) + rows(denv[ks], 8))
        for t, x in enumerate((r, dr)):
            hi = x.astype(bf16).astype(f32)
            y = jnp.concatenate([hi, x - hi], axis=0).astype(bf16)
            radf[k, t] = jnp.concatenate([y, y], axis=0)

def radial_maps(w, radf, t, first, n):
    y = dot(w, jnp.concatenate([radf[first + i, t] for i in range(n)], axis=1))
    return [y[:, 128 * i:128 * i + 128] for i in range(n)]


def all_radial_maps(rwt, radf, S):
    w = rwt[...]

    def step(i, _):
        for kk, y in enumerate(radial_maps(w, radf, 0, 8 * i, 8)):
            for l in range(3):
                S[l, 8 * i + kk] = y[l * 128:l * 128 + 128]
        return 0

    lax.fori_loop(0, K // 8, step, 0)


def amplitudes(G, S, angb, amp):
    def tile(ci, _):
        cs = pl.ds(pl.multiple_of(ci * 16, 16), 16)
        def step(k, acc):
            g = G[k, cs]
            h = []
            for l in range(3):
                x = g * S[l, k, cs]
                S[l, k, cs] = x
                h.append(x)
            out = [acc[0] + h[0]]
            for m in range(8):
                a = angb[m, k]
                a = jnp.concatenate([a, a], axis=0)
                out.append(acc[m + 1] + a * h[1 if m < 3 else 2])
            return tuple(out)
        acc = lax.fori_loop(0, K, step, tuple(jnp.zeros((16, A), f32) for _ in range(9)), unroll=8)
        for m in range(9):
            amp[m, cs] = acc[m]
        return 0
    lax.fori_loop(0, C // 16, tile, 0)

def readout(amp, mixt, mixn, rot, ron, rvc, sws, own, energy_ref):
    mixed = []
    for l, (lo, hi) in enumerate(((0, 1), (1, 4), (4, 9))):
        x = jnp.concatenate([amp[m] * 0.25 for m in range(lo, hi)], axis=1)
        y = dot(mixt[l], stack3(x))
        mixed += [y[:, 128 * i:128 * i + 128] for i in range(hi - lo)]
    inv = [mixed[0],
           mixed[1] * mixed[1] + mixed[2] * mixed[2] + mixed[3] * mixed[3],
           mixed[4] * mixed[4] + mixed[5] * mixed[5] + mixed[6] * mixed[6] + mixed[7] * mixed[7] + mixed[8] * mixed[8]]
    t = dot(rot[0], stack3(inv[0])) + dot(rot[1], stack3(inv[1])) + dot(rot[2], stack3(inv[2]))
    sg = 1.0 / (1.0 + jnp.exp(-t))
    self_e = dot(sws[...], own)
    energy_ref[...] = jnp.sum(rvc[...] * (t * sg), axis=0, keepdims=True) + jnp.sum(self_e, axis=0, keepdims=True)
    dh = rvc[...] * (sg * (1.0 + t * (1.0 - sg)))
    dinv = dot(ron[...], stack3(dh))
    d = [dinv[0:128], dinv[128:256] * 2.0, dinv[256:384] * 2.0]
    for l, (lo, hi) in enumerate(((0, 1), (1, 4), (4, 9))):
        x = jnp.concatenate([d[l] if l == 0 else d[l] * mixed[m] for m in range(lo, hi)], axis=1)
        y = dot(mixn[l], stack3(x)) * 0.25
        for i in range(hi - lo):
            amp[lo + i] = y[:, 128 * i:128 * i + 128]

def edge_gradients(G, S, Da, Db, rwt, radf, angb, damp, dA):
    w = rwt[...]

    def maps(chunk, dst):
        for kk, y in enumerate(radial_maps(w, radf, 1, 4 * chunk, 4)):
            for l in range(3):
                dst[l, kk] = y[l * 128:l * 128 + 128]

    def edges(chunk, dS):
        for kk in range(0, 4, 2):
            ks = [4 * chunk + kk, 4 * chunk + kk + 1]
            a = [[angb[m, k] for m in range(8)] for k in ks]
            acc = [[jnp.zeros((8, A), f32) for _ in range(9)] for _ in ks]
            for ci in range(16):
                cs = slice(8 * ci, 8 * ci + 8)
                dm = [damp[m, cs] for m in range(9)]
                for j, k in enumerate(ks):
                    h1, h2 = S[1, k, cs], S[2, k, cs]
                    b = a[j]
                    for m in range(8):
                        acc[j][m + 1] = acc[j][m + 1] + (h1 if m < 3 else h2) * dm[m + 1]
                    t1 = b[0] * dm[1] + b[1] * dm[2] + b[2] * dm[3]
                    t2 = (b[3] * dm[4] + b[4] * dm[5]) + (b[5] * dm[6] + b[6] * dm[7]) + b[7] * dm[8]
                    acc[j][0] = acc[j][0] + G[k, cs] * (
                        dS[0, kk + j, cs] * dm[0] + dS[1, kk + j, cs] * t1 + dS[2, kk + j, cs] * t2)
            for j, k in enumerate(ks):
                for m in range(9):
                    dA[m, pl.ds(k, 1)] = jnp.sum(acc[j][m], axis=0, keepdims=True)

    maps(0, Da)

    def step(i, _):
        maps(2 * i + 1, Db)
        edges(2 * i, Da)
        maps(jnp.minimum(2 * i + 2, 7), Da)
        edges(2 * i + 1, Db)
        return 0

    lax.fori_loop(0, 4, step, 0)


def forces_out(ids_ref, rel, dA, D):
    u, v, w = rel[0], rel[1], rel[2]
    dS, d1, d2, d3, d4, d5, d6, d7, d8 = [dA[m] for m in range(9)]
    base = 2.0 * dS - R5 * d6
    gu = base * u + R3 * d1 + R15 * (v * d4 + w * d7 + u * d8)
    gv = base * v + R3 * d2 + R15 * (u * d4 + w * d5 - v * d8)
    gw = 2.0 * w * (dS + R5 * d6) + R3 * d3 + R15 * (v * d5 + u * d7)
    g = [gu, gv, gw]
    parts = []
    for x in g:
        hi = x.astype(bf16).astype(f32)
        parts += [hi, x - hi]
    ii = lax.broadcasted_iota(i32, (8, A), 0)
    iot = lax.broadcasted_iota(i32, (16, A), 0)
    acc = None
    ids = ids_ref[...]
    for c in range(0, K, 2):
        lhs, rhs = [], []
        for k in (c, c + 1):
            x = jnp.zeros((8, A), f32)
            for j, (p, r) in enumerate(((0, 0), (2, 1), (4, 2), (1, 4), (3, 5), (5, 6))):
                x = jnp.where(ii == r, rows(parts[p][k:k + 1], 8), x)
            idr = rows(ids[k:k + 1], 8)
            qk = idr >> 7
            col = [jnp.where(qk == b, x, 0.0) for b in range(27)] + [jnp.zeros((8, A), f32)]
            lhs.append(jnp.concatenate(col, axis=0).astype(bf16))
            s = rows(ids[k:k + 1], 16) & 127
            rhs.append(jnp.concatenate([jnp.where(s == iot + 16 * r, 1.0, 0.0).astype(bf16) for r in range(8)], axis=0))
        y = dot_nt(jnp.concatenate(lhs, axis=1), jnp.concatenate(rhs, axis=1))
        acc = y if acc is None else acc + y
    for b in range(27):
        y = acc[8 * b:8 * b + 8]
        D[SLOT_OF[b]] = y[0:4] + y[4:8] if b != 13 else y[0:4] + y[4:8] - jnp.concatenate([jnp.sum(x, axis=0, keepdims=True) for x in g] + [jnp.zeros((1, A), f32)], axis=0)

MESH = pl.DeviceIdType.MESH
def bin_of(h):
    return (h // 3 % 3) * 9 + (h % 3) * 3 + h // 9


HALO_OF = {bin_of(h): h for h in range(27)}
AROUND = tuple(h for h in range(27) if h != 13)
SLOT = {h: i for i, h in enumerate(AROUND + (13,))}
SLOT_OF = {bin_of(h): i for h, i in SLOT.items()}


def distance(h):
    return -sum(i != 1 for i in (h // 9, h // 3 % 3, h % 3))


def gather_chunk(ids_ref, feat, blocks, chunk, n):
    iot = lax.broadcasted_iota(i32, (16, A), 0)
    slots, qs = [], []
    for kk in range(n):
        row = jnp.broadcast_to(ids_ref[pl.ds(n * chunk + kk, 1), :], (16, A))
        qs.append((row >> 7).astype(i16))
        s = row & 127
        slots.append([jnp.where(s == iot + 16 * r, 1.0, 0.0).astype(bf16) for r in range(8)])
    zero = jnp.zeros((16, A), bf16)
    acc = None
    for t in range(0, len(blocks), 2):
        pair = blocks[t:t + 2]
        cols = []
        for kk in range(n):
            pieces = []
            for h in pair:
                m = qs[kk] == jnp.int16(bin_of(h))
                pieces += [jnp.where(m, slots[kk][r], zero) for r in range(8)]
            cols.append(jnp.concatenate(pieces, axis=0))
        y = dot(jnp.concatenate([feat[h] for h in pair], axis=1), jnp.concatenate(cols, axis=1))
        acc = y if acc is None else acc + y
    return [acc[:, kk * 128:kk * 128 + 128] for kk in range(n)]


def gather(ids_ref, feat, G, blocks, first, n=8):
    def step(i, _):
        for kk, y in enumerate(gather_chunk(ids_ref, feat, blocks, i, n)):
            G[n * i + kk] = y if first else G[n * i + kk] + y
        return 0

    lax.fori_loop(0, K // n, step, 0)


def kernel(sizes, f_hbm, p_hbm, ids_hbm, cnt_hbm, rw_hbm, mix_hbm, ro_hbm, rv_hbm, sw_hbm, en_ref, out_ref,
           f_ref, p_ref, ids_ref, cnt_ref, rw_ref, mix_ref, ro_ref, rv_ref, sw_ref,
           feat, hpos, rwt, mixt, mixn, rot, ron, rvc, sws, rel, angb, radf, S, G, Da, Db, amp, dA,
           D, landing, ls, fs, fr, ps, pr, bs, br):
    place = {}
    for axis in sizes:
        me, size = lax.axis_index(axis), sizes[axis]
        place[axis] = (jnp.where(me == 0, size - 1, me - 1), me, jnp.where(me == size - 1, 0, me + 1))

    def device(h):
        return {"gx": place["gx"][h // 3 % 3], "gy": place["gy"][h % 3], "gz": place["gz"][h // 9]}

    def remote(h, src, dst, send, recv):
        return pltpu.make_async_remote_copy(src_ref=src, dst_ref=dst, send_sem=send, recv_sem=recv,
                                            device_id=device(h), device_id_type=MESH)

    plane = (10, 16, 12, 14, 9, 11, 15, 17)
    barrier = pltpu.get_barrier_semaphore()
    for h in (4, 22) + plane:
        pl.semaphore_signal(barrier, inc=1, device_id=device(h), device_id_type=MESH)
    local = [pltpu.make_async_copy(src, dst, ls.at[i]) for i, (src, dst) in enumerate((
        (f_hbm, f_ref), (p_hbm, p_ref), (rw_hbm, rw_ref), (mix_hbm, mix_ref), (ro_hbm, ro_ref), (rv_hbm, rv_ref),
        (sw_hbm, sw_ref), (ids_hbm, ids_ref), (cnt_hbm, cnt_ref)))]
    for copy in local:
        copy.start()
    local[0].wait()
    local[1].wait()
    feat[13] = f_ref[...].astype(f32).T.astype(bf16)
    hpos[13] = jnp.concatenate([p_ref[...].astype(f32), jnp.zeros((13, A), f32)], axis=0).astype(bf16)
    pl.semaphore_wait(barrier, 10)

    pos = [remote(h, hpos.at[13], hpos.at[26 - h], ps.at[i], pr.at[i]) for i, h in enumerate(plane)]
    pos_z = [remote(h, hpos.at[pl.ds(9, 9)], hpos.at[pl.ds(18 - h // 9 * 9, 9)], ps.at[8 + i], pr.at[8 + i])
             for i, h in enumerate((4, 22))]
    feat_y = [remote(h, feat.at[13], feat.at[26 - h], fs.at[i], fr.at[i]) for i, h in enumerate((12, 14))]
    feat_x = [remote(h, feat.at[pl.ds(12, 3)], feat.at[pl.ds(24 - (h - 1), 3)], fs.at[2 + i], fr.at[2 + i])
              for i, h in enumerate((10, 16))]
    odd = lax.rem(place["gx"][1], 2)
    outer, inner = 6 * odd, 6 - 6 * odd
    feat_z = [remote(h, feat.at[pl.ds(12, 3)], feat.at[pl.ds(21 - h // 9 * 9, 3)], fs.at[4 + i], fr.at[4 + i])
              for i, h in enumerate((4, 22))]
    feat_o = [remote(h, feat.at[pl.ds(9 + outer, 3)], feat.at[pl.ds(18 - h // 9 * 9 + outer, 3)], fs.at[6 + i], fr.at[6 + i])
              for i, h in enumerate((4, 22))]

    def share(row):
        return [pltpu.make_async_remote_copy(
            src_ref=feat.at[pl.ds(z + 3, 3)], dst_ref=feat.at[pl.ds(z + row, 3)], send_sem=fs.at[8 + i], recv_sem=fr.at[8 + i],
            device_id={"gx": place["gx"][1] + 1 - 2 * odd, "gy": place["gy"][1], "gz": place["gz"][1]}, device_id_type=MESH)
            for i, z in enumerate((0, 18))]

    feat_s = share(outer)

    def start(copies):
        for copy in copies:
            copy.start()

    def arrive(copies):
        for copy in copies:
            copy.wait_recv()

    start(pos)
    start(feat_y)
    arrive(pos)
    start(pos_z)
    arrive(feat_y)
    start(feat_x)
    start(feat_z)
    for copy in local[2:]:
        copy.wait()
    prepare_weights(rw_ref, mix_ref, ro_ref, rv_ref, sw_ref, rwt, mixt, mixn, rot, ron, rvc, sws)
    arrive(pos_z)
    geometry(ids_ref, cnt_ref, hpos, rel, angb, radf)
    arrive(feat_x)
    start(feat_o)
    arrive(feat_z)
    start(feat_s)
    all_radial_maps(rwt, radf, S)
    gather(ids_ref, feat, G, tuple(range(9, 18)), True)
    gather(ids_ref, feat, G, (3, 4, 5, 21, 22, 23), False)
    arrive(feat_o)
    arrive(share(inner))
    gather(ids_ref, feat, G, (0, 1, 2, 6, 7, 8, 18, 19, 20, 24, 25, 26), False)
    amplitudes(G, S, angb, amp)
    readout(amp, mixt, mixn, rot, ron, rvc, sws, feat[13], en_ref)
    edge_gradients(G, S, Da, Db, rwt, radf, angb, amp, dA)
    forces_out(ids_ref, rel, dA, D)

    start([remote(h, D.at[SLOT[h]], landing.at[SLOT[26 - h]], bs.at[0], br.at[0]) for h in sorted(AROUND, key=distance)])
    for copy in pos + pos_z + feat_y + feat_x + feat_z + feat_o + feat_s:
        copy.wait_send()
    every = pl.ds(0, 26)
    pltpu.make_async_copy(landing.at[every], landing.at[every], br.at[0]).wait()
    total = D[26]
    for i in range(26):
        total = total + landing[i]
    out_ref[...] = -total[0:3]
    pltpu.make_async_copy(D.at[every], D.at[every], bs.at[0]).wait()


def solution(mesh):
    sizes = dict(mesh.shape)
    V, DMA = pltpu.VMEM, pltpu.SemaphoreType.DMA

    def body(features, positions, ids, counts, rw, mix, ro, rv, sw):
        energy, forces = pl.pallas_call(
            lambda *refs: kernel(sizes, *refs),
            out_shape=(jax.ShapeDtypeStruct((1, A), f32), jax.ShapeDtypeStruct((3, A), f32)),
            in_specs=[pl.BlockSpec(memory_space=pltpu.HBM)] * 9,
            scratch_shapes=[
                V((A, C), bf16), V((3, A), bf16), V((K, A), i32), V((1, A), i32), V((J, 384), f32), V((3, C, C), f32),
                V((H, 384), f32), V((1, H), f32), V((1, C), f32),
                V((27, C, A), bf16), V((27, 16, A), bf16), V((384, 32), bf16), V((3, C, 384), bf16), V((3, C, 384), bf16),
                V((3, H, 384), bf16), V((384, 48), bf16), V((H, A), f32), V((16, C), bf16), V((3, K, A), f32),
                V((8, K, 8, A), f32), V((K, 2, 32, A), bf16), V((3, K, C, A), f32), V((K, C, A), f32),
                V((3, 4, C, A), f32), V((3, 4, C, A), f32), V((9, C, A), f32),
                V((9, K, A), f32), V((27, 4, A), f32), V((26, 4, A), f32),
                DMA((9,)), DMA((10,)), DMA((10,)), DMA((10,)), DMA((10,)), DMA((1,)), DMA((1,)),
            ],
            compiler_params=pltpu.CompilerParams(collective_id=0, has_side_effects=True, vmem_limit_bytes=48 * 2**20),
        )(*(pltpu.with_memory_space_constraint(x, pltpu.HBM) for x in (
            features.reshape(A, C), positions.reshape(3, A), ids.reshape(K, A), counts.reshape(1, A), rw, mix, ro.T,
            rv.reshape(1, H), sw.reshape(1, C))))
        return energy.reshape(1, 1, 1, A), forces.reshape(1, 1, 1, 3, A)

    block = ("gx", "gy", "gz")
    in_specs = (P(*block, None, None),) * 3 + (P(*block, None),) + (P(),) * 5
    out_specs = (P(*block, None), P(*block, None, None))
    return jax.shard_map(body, mesh=mesh, in_specs=in_specs, out_specs=out_specs, check_vma=False)
```

```python
import functools, math
HALO_OF = {b: b for b in range(27)}
import jax, jax.numpy as jnp
from jax import lax
from jax.experimental import pallas as pl
from jax.experimental.pallas import tpu as pltpu
from jax.sharding import PartitionSpec as P

C = 128; A = 128; K = 32; J = 8; H = 16
f32, bf16, i32, i16 = jnp.float32, jnp.bfloat16, jnp.int32, jnp.int16
R3, R5, R15 = math.sqrt(3.0), math.sqrt(5.0), math.sqrt(15.0)

def split(x):
    hi = x.astype(bf16)
    return hi, (x - hi.astype(f32)).astype(bf16)

def dot(a, b):
    return jnp.dot(a, b, preferred_element_type=f32)

def dot_nt(a, b):
    return lax.dot_general(a, b, (((1,), (1,)), ((), ())), preferred_element_type=f32)

def rows(x, n):
    return jnp.broadcast_to(x, (n, x.shape[1]))

def prepare_weights(rw_ref, mix_ref, ro_ref, rv_ref, sw_ref, rwt, mixt, mixn, rot, ron, rvc, sws):
    hi, lo = split(rw_ref[...])
    hi, lo = hi.astype(f32), lo.astype(f32)
    pad = jnp.zeros((96, 128), f32)
    for l in range(3):
        s = slice(l * 128, l * 128 + 128)
        x = jnp.concatenate([hi[:, s], hi[:, s], lo[:, s], lo[:, s], pad], axis=0)
        rwt[s, :] = x.T[:, :32].astype(bf16)
    for l in range(3):
        m = mix_ref[l]
        h, w = split(m.T)
        mixt[l, :, :] = jnp.concatenate([h, h, w], axis=1)
        h, w = split(m)
        mixn[l, :, :] = jnp.concatenate([h, h, w], axis=1)
    for l in range(3):
        s = slice(l * 128, l * 128 + 128)
        x = ro_ref[:, s]
        h, w = split(x)
        rot[l, :, :] = jnp.concatenate([h, h, w], axis=1)
        h, w = split(jnp.concatenate([x, jnp.zeros((112, 128), f32)], axis=0).T[:, :16])
        ron[s, :] = jnp.concatenate([h, h, w], axis=1)
    rvc[...] = jnp.broadcast_to(rv_ref[...], (128, 16)).T
    h, w = split(sw_ref[...])
    w2 = (sw_ref[...] - h.astype(f32) - w.astype(f32)).astype(bf16)
    ii = lax.broadcasted_iota(i32, (16, 128), 0)
    sws[...] = jnp.where(ii == 0, rows(h.astype(f32), 16), jnp.where(ii == 1, rows(w.astype(f32), 16), jnp.where(ii == 2, rows(w2.astype(f32), 16), 0.0))).astype(bf16)

def stack3(x):
    h, w = split(x)
    return jnp.concatenate([h, w, h], axis=0)

def geometry(ids_ref, cnt_ref, pos, rel, angb, radf):
    ids = ids_ref[...]
    q = ids >> 7
    slot = ids & 127
    acc = [jnp.zeros((K, A), f32) for _ in range(3)]
    for b in range(27):
        p = pos[HALO_OF[b]].astype(f32)
        m = q == b
        for c in range(3):
            t = jnp.take_along_axis(jnp.broadcast_to(p[c:c + 1], (K, A)), slot, axis=1)
            acc[c] = jnp.where(m, t, acc[c])
    q9 = (q * 57) >> 9
    q3 = (q * 43) >> 7
    off = [q9 - 1, q3 - 3 * q9 - 1, q - 3 * q3 - 1]
    own = pos[13].astype(f32)
    u, v, w = [(acc[c] + off[c].astype(f32)) - own[c:c + 1] for c in range(3)]
    sq = u * u + v * v + w * w
    rel[0] = u; rel[1] = v; rel[2] = w
    live = (lax.broadcasted_iota(i32, (K, A), 0) < cnt_ref[...]).astype(f32)
    e1 = 1.0 - sq / 16.0
    env = e1 * e1 * live
    denv = e1 * live * (-0.125)
    ang = [R3 * u, R3 * v, R3 * w, R15 * u * v, R15 * v * w, 0.5 * R5 * (3.0 * w * w - sq), R15 * u * w, 0.5 * R15 * (u * u - v * v)]
    decay = -0.08 * jnp.left_shift(1, lax.broadcasted_iota(i32, (J, A), 0)).astype(f32)
    for k in range(K):
        ks = slice(k, k + 1)
        for m in range(8):
            angb[m, k] = rows(ang[m][ks], 8)
        ex = jnp.exp(decay * rows(sq[ks], 8))
        r = ex * rows(env[ks], 8)
        dr = ex * (decay * rows(env[ks], 8) + rows(denv[ks], 8))
        for t, x in enumerate((r, dr)):
            hi = x.astype(bf16).astype(f32)
            y = jnp.concatenate([hi, x - hi], axis=0).astype(bf16)
            radf[k, t] = jnp.concatenate([y, y], axis=0)

def radial_maps(w, radf, t, first, n):
    y = dot(w, jnp.concatenate([radf[first + i, t] for i in range(n)], axis=1))
    return [y[:, 128 * i:128 * i + 128] for i in range(n)]


def all_radial_maps(rwt, radf, S):
    w = rwt[...]

    def step(i, _):
        for kk, y in enumerate(radial_maps(w, radf, 0, 8 * i, 8)):
            for l in range(3):
                S[l, 8 * i + kk] = y[l * 128:l * 128 + 128]
        return 0

    lax.fori_loop(0, K // 8, step, 0)


def amplitudes(G, S, angb, amp):
    def tile(ci, _):
        cs = pl.ds(pl.multiple_of(ci * 16, 16), 16)
        def step(k, acc):
            g = G[k, cs]
            h = []
            for l in range(3):
                x = g * S[l, k, cs]
                S[l, k, cs] = x
                h.append(x)
            out = [acc[0] + h[0]]
            for m in range(8):
                a = angb[m, k]
                a = jnp.concatenate([a, a], axis=0)
                out.append(acc[m + 1] + a * h[1 if m < 3 else 2])
            return tuple(out)
        acc = lax.fori_loop(0, K, step, tuple(jnp.zeros((16, A), f32) for _ in range(9)), unroll=16)
        for m in range(9):
            amp[m, cs] = acc[m]
        return 0
    lax.fori_loop(0, C // 16, tile, 0)

def readout(amp, mixt, mixn, rot, ron, rvc, sws, own, energy_ref):
    mixed = []
    for l, (lo, hi) in enumerate(((0, 1), (1, 4), (4, 9))):
        x = jnp.concatenate([amp[m] * 0.25 for m in range(lo, hi)], axis=1)
        y = dot(mixt[l], stack3(x))
        mixed += [y[:, 128 * i:128 * i + 128] for i in range(hi - lo)]
    inv = [mixed[0],
           mixed[1] * mixed[1] + mixed[2] * mixed[2] + mixed[3] * mixed[3],
           mixed[4] * mixed[4] + mixed[5] * mixed[5] + mixed[6] * mixed[6] + mixed[7] * mixed[7] + mixed[8] * mixed[8]]
    t = dot(rot[0], stack3(inv[0])) + dot(rot[1], stack3(inv[1])) + dot(rot[2], stack3(inv[2]))
    sg = 1.0 / (1.0 + jnp.exp(-t))
    self_e = dot(sws[...], own)
    energy_ref[...] = jnp.sum(rvc[...] * (t * sg), axis=0, keepdims=True) + jnp.sum(self_e, axis=0, keepdims=True)
    dh = rvc[...] * (sg * (1.0 + t * (1.0 - sg)))
    dinv = dot(ron[...], stack3(dh))
    d = [dinv[0:128], dinv[128:256] * 2.0, dinv[256:384] * 2.0]
    for l, (lo, hi) in enumerate(((0, 1), (1, 4), (4, 9))):
        x = jnp.concatenate([d[l] if l == 0 else d[l] * mixed[m] for m in range(lo, hi)], axis=1)
        y = dot(mixn[l], stack3(x)) * 0.25
        for i in range(hi - lo):
            amp[lo + i] = y[:, 128 * i:128 * i + 128]

def edge_gradients(G, S, Da, Db, rwt, radf, angb, damp, dA):
    w = rwt[...]

    def maps(chunk, dst):
        for kk, y in enumerate(radial_maps(w, radf, 1, 4 * chunk, 4)):
            for l in range(3):
                dst[l, kk] = y[l * 128:l * 128 + 128]

    def edges(chunk, dS):
        for kk in range(0, 4, 2):
            ks = [4 * chunk + kk, 4 * chunk + kk + 1]
            a = [[angb[m, k] for m in range(8)] for k in ks]
            acc = [[jnp.zeros((8, A), f32) for _ in range(9)] for _ in ks]
            for ci in range(16):
                cs = slice(8 * ci, 8 * ci + 8)
                dm = [damp[m, cs] for m in range(9)]
                for j, k in enumerate(ks):
                    h1, h2 = S[1, k, cs], S[2, k, cs]
                    b = a[j]
                    for m in range(8):
                        acc[j][m + 1] = acc[j][m + 1] + (h1 if m < 3 else h2) * dm[m + 1]
                    t1 = b[0] * dm[1] + b[1] * dm[2] + b[2] * dm[3]
                    t2 = (b[3] * dm[4] + b[4] * dm[5]) + (b[5] * dm[6] + b[6] * dm[7]) + b[7] * dm[8]
                    acc[j][0] = acc[j][0] + G[k, cs] * (
                        dS[0, kk + j, cs] * dm[0] + dS[1, kk + j, cs] * t1 + dS[2, kk + j, cs] * t2)
            for j, k in enumerate(ks):
                for m in range(9):
                    dA[m, pl.ds(k, 1)] = jnp.sum(acc[j][m], axis=0, keepdims=True)

    maps(0, Da)

    def step(i, _):
        maps(2 * i + 1, Db)
        edges(2 * i, Da)
        maps(jnp.minimum(2 * i + 2, 7), Da)
        edges(2 * i + 1, Db)
        return 0

    lax.fori_loop(0, 4, step, 0)


def forces_out(ids_ref, rel, dA, D):
    u, v, w = rel[0], rel[1], rel[2]
    dS, d1, d2, d3, d4, d5, d6, d7, d8 = [dA[m] for m in range(9)]
    base = 2.0 * dS - R5 * d6
    gu = base * u + R3 * d1 + R15 * (v * d4 + w * d7 + u * d8)
    gv = base * v + R3 * d2 + R15 * (u * d4 + w * d5 - v * d8)
    gw = 2.0 * w * (dS + R5 * d6) + R3 * d3 + R15 * (v * d5 + u * d7)
    g = [gu, gv, gw]
    parts = []
    for x in g:
        hi = x.astype(bf16).astype(f32)
        parts += [hi, x - hi]
    ii = lax.broadcasted_iota(i32, (8, A), 0)
    iot = lax.broadcasted_iota(i32, (16, A), 0)
    acc = None
    ids = ids_ref[...]
    for c in range(0, K, 2):
        lhs, rhs = [], []
        for k in (c, c + 1):
            x = jnp.zeros((8, A), f32)
            for j, (p, r) in enumerate(((0, 0), (2, 1), (4, 2), (1, 4), (3, 5), (5, 6))):
                x = jnp.where(ii == r, rows(parts[p][k:k + 1], 8), x)
            idr = rows(ids[k:k + 1], 8)
            qk = idr >> 7
            col = [jnp.where(qk == b, x, 0.0) for b in range(27)] + [jnp.zeros((8, A), f32)]
            lhs.append(jnp.concatenate(col, axis=0).astype(bf16))
            s = rows(ids[k:k + 1], 16) & 127
            rhs.append(jnp.concatenate([jnp.where(s == iot + 16 * r, 1.0, 0.0).astype(bf16) for r in range(8)], axis=0))
        y = dot_nt(jnp.concatenate(lhs, axis=1), jnp.concatenate(rhs, axis=1))
        acc = y if acc is None else acc + y
    for b in range(27):
        y = acc[8 * b:8 * b + 8]
        D[SLOT_OF[b]] = y[0:4] + y[4:8] if b != 13 else y[0:4] + y[4:8] - jnp.concatenate([jnp.sum(x, axis=0, keepdims=True) for x in g] + [jnp.zeros((1, A), f32)], axis=0)

MESH = pl.DeviceIdType.MESH
def bin_of(h):
    return (h // 3 % 3) * 9 + (h % 3) * 3 + h // 9


HALO_OF = {bin_of(h): h for h in range(27)}
AROUND = tuple(h for h in range(27) if h != 13)
SLOT = {h: i for i, h in enumerate(AROUND + (13,))}
SLOT_OF = {bin_of(h): i for h, i in SLOT.items()}


def distance(h):
    return -sum(i != 1 for i in (h // 9, h // 3 % 3, h % 3))


def gather_chunk(ids_ref, feat, blocks, chunk, n):
    iot = lax.broadcasted_iota(i32, (16, A), 0)
    slots, qs = [], []
    for kk in range(n):
        row = jnp.broadcast_to(ids_ref[pl.ds(n * chunk + kk, 1), :], (16, A))
        qs.append((row >> 7).astype(i16))
        s = row & 127
        slots.append([jnp.where(s == iot + 16 * r, 1.0, 0.0).astype(bf16) for r in range(8)])
    zero = jnp.zeros((16, A), bf16)
    acc = None
    for t in range(0, len(blocks), 2):
        pair = blocks[t:t + 2]
        cols = []
        for kk in range(n):
            pieces = []
            for h in pair:
                m = qs[kk] == jnp.int16(bin_of(h))
                pieces += [jnp.where(m, slots[kk][r], zero) for r in range(8)]
            cols.append(jnp.concatenate(pieces, axis=0))
        y = dot(jnp.concatenate([feat[h] for h in pair], axis=1), jnp.concatenate(cols, axis=1))
        acc = y if acc is None else acc + y
    return [acc[:, kk * 128:kk * 128 + 128] for kk in range(n)]


def gather(ids_ref, feat, G, blocks, first, n=32):
    def step(i, _):
        for kk, y in enumerate(gather_chunk(ids_ref, feat, blocks, i, n)):
            G[n * i + kk] = y if first else G[n * i + kk] + y
        return 0

    lax.fori_loop(0, K // n, step, 0)


def kernel(sizes, f_hbm, p_hbm, ids_hbm, cnt_hbm, rw_hbm, mix_hbm, ro_hbm, rv_hbm, sw_hbm, en_ref, out_ref,
           f_ref, p_ref, ids_ref, cnt_ref, rw_ref, mix_ref, ro_ref, rv_ref, sw_ref,
           feat, hpos, rwt, mixt, mixn, rot, ron, rvc, sws, rel, angb, radf, S, G, Da, Db, amp, dA,
           D, landing, ls, fs, fr, ps, pr, bs, br):
    place = {}
    for axis in sizes:
        me, size = lax.axis_index(axis), sizes[axis]
        place[axis] = (jnp.where(me == 0, size - 1, me - 1), me, jnp.where(me == size - 1, 0, me + 1))

    def device(h):
        return {"gx": place["gx"][h // 3 % 3], "gy": place["gy"][h % 3], "gz": place["gz"][h // 9]}

    def remote(h, src, dst, send, recv):
        return pltpu.make_async_remote_copy(src_ref=src, dst_ref=dst, send_sem=send, recv_sem=recv,
                                            device_id=device(h), device_id_type=MESH)

    plane = (10, 16, 12, 14, 9, 11, 15, 17)
    barrier = pltpu.get_barrier_semaphore()
    for h in (4, 22) + plane:
        pl.semaphore_signal(barrier, inc=1, device_id=device(h), device_id_type=MESH)
    local = [pltpu.make_async_copy(src, dst, ls.at[i]) for i, (src, dst) in enumerate((
        (f_hbm, f_ref), (p_hbm, p_ref), (rw_hbm, rw_ref), (mix_hbm, mix_ref), (ro_hbm, ro_ref), (rv_hbm, rv_ref),
        (sw_hbm, sw_ref), (ids_hbm, ids_ref), (cnt_hbm, cnt_ref)))]
    for copy in local:
        copy.start()
    local[0].wait()
    local[1].wait()
    feat[13] = f_ref[...].astype(f32).T.astype(bf16)
    hpos[13] = jnp.concatenate([p_ref[...].astype(f32), jnp.zeros((13, A), f32)], axis=0).astype(bf16)
    pl.semaphore_wait(barrier, 10)

    pos = [remote(h, hpos.at[13], hpos.at[26 - h], ps.at[i], pr.at[i]) for i, h in enumerate(plane)]
    pos_z = [remote(h, hpos.at[pl.ds(9, 9)], hpos.at[pl.ds(18 - h // 9 * 9, 9)], ps.at[8 + i], pr.at[8 + i])
             for i, h in enumerate((4, 22))]
    feat_y = [remote(h, feat.at[13], feat.at[26 - h], fs.at[i], fr.at[i]) for i, h in enumerate((12, 14))]
    feat_x = [remote(h, feat.at[pl.ds(12, 3)], feat.at[pl.ds(24 - (h - 1), 3)], fs.at[2 + i], fr.at[2 + i])
              for i, h in enumerate((10, 16))]
    odd = lax.rem(place["gx"][1], 2)
    outer, inner = 6 * odd, 6 - 6 * odd
    feat_z = [remote(h, feat.at[pl.ds(12, 3)], feat.at[pl.ds(21 - h // 9 * 9, 3)], fs.at[4 + i], fr.at[4 + i])
              for i, h in enumerate((4, 22))]
    feat_o = [remote(h, feat.at[pl.ds(9 + outer, 3)], feat.at[pl.ds(18 - h // 9 * 9 + outer, 3)], fs.at[6 + i], fr.at[6 + i])
              for i, h in enumerate((4, 22))]

    def share(row):
        return [pltpu.make_async_remote_copy(
            src_ref=feat.at[pl.ds(z + 3, 3)], dst_ref=feat.at[pl.ds(z + row, 3)], send_sem=fs.at[8 + i], recv_sem=fr.at[8 + i],
            device_id={"gx": place["gx"][1] + 1 - 2 * odd, "gy": place["gy"][1], "gz": place["gz"][1]}, device_id_type=MESH)
            for i, z in enumerate((0, 18))]

    feat_s = share(outer)

    def start(copies):
        for copy in copies:
            copy.start()

    def arrive(copies):
        for copy in copies:
            copy.wait_recv()

    start(pos)
    start(feat_y)
    arrive(pos)
    start(pos_z)
    arrive(feat_y)
    start(feat_x)
    start(feat_z)
    for copy in local[2:]:
        copy.wait()
    prepare_weights(rw_ref, mix_ref, ro_ref, rv_ref, sw_ref, rwt, mixt, mixn, rot, ron, rvc, sws)
    arrive(pos_z)
    geometry(ids_ref, cnt_ref, hpos, rel, angb, radf)
    arrive(feat_x)
    start(feat_o)
    arrive(feat_z)
    start(feat_s)
    all_radial_maps(rwt, radf, S)
    gather(ids_ref, feat, G, tuple(range(9, 18)), True)
    gather(ids_ref, feat, G, (3, 4, 5, 21, 22, 23), False)
    arrive(feat_o)
    arrive(share(inner))
    gather(ids_ref, feat, G, (0, 1, 2, 6, 7, 8, 18, 19, 20, 24, 25, 26), False)
    amplitudes(G, S, angb, amp)
    readout(amp, mixt, mixn, rot, ron, rvc, sws, feat[13], en_ref)
    edge_gradients(G, S, Da, Db, rwt, radf, angb, amp, dA)
    forces_out(ids_ref, rel, dA, D)

    start([remote(h, D.at[SLOT[h]], landing.at[SLOT[26 - h]], bs.at[0], br.at[0]) for h in sorted(AROUND, key=distance)])
    for copy in pos + pos_z + feat_y + feat_x + feat_z + feat_o + feat_s:
        copy.wait_send()
    every = pl.ds(0, 26)
    pltpu.make_async_copy(landing.at[every], landing.at[every], br.at[0]).wait()
    total = D[26]
    for i in range(26):
        total = total + landing[i]
    out_ref[...] = -total[0:3]
    pltpu.make_async_copy(D.at[every], D.at[every], bs.at[0]).wait()


def solution(mesh):
    sizes = dict(mesh.shape)
    V, DMA = pltpu.VMEM, pltpu.SemaphoreType.DMA

    def body(features, positions, ids, counts, rw, mix, ro, rv, sw):
        energy, forces = pl.pallas_call(
            lambda *refs: kernel(sizes, *refs),
            out_shape=(jax.ShapeDtypeStruct((1, A), f32), jax.ShapeDtypeStruct((3, A), f32)),
            in_specs=[pl.BlockSpec(memory_space=pltpu.HBM)] * 9,
            scratch_shapes=[
                V((A, C), bf16), V((3, A), bf16), V((K, A), i32), V((1, A), i32), V((J, 384), f32), V((3, C, C), f32),
                V((H, 384), f32), V((1, H), f32), V((1, C), f32),
                V((27, C, A), bf16), V((27, 16, A), bf16), V((384, 32), bf16), V((3, C, 384), bf16), V((3, C, 384), bf16),
                V((3, H, 384), bf16), V((384, 48), bf16), V((H, A), f32), V((16, C), bf16), V((3, K, A), f32),
                V((8, K, 8, A), f32), V((K, 2, 32, A), bf16), V((3, K, C, A), f32), V((K, C, A), f32),
                V((3, 4, C, A), f32), V((3, 4, C, A), f32), V((9, C, A), f32),
                V((9, K, A), f32), V((27, 4, A), f32), V((26, 4, A), f32),
                DMA((9,)), DMA((10,)), DMA((10,)), DMA((10,)), DMA((10,)), DMA((1,)), DMA((1,)),
            ],
            compiler_params=pltpu.CompilerParams(collective_id=0, has_side_effects=True, vmem_limit_bytes=48 * 2**20),
        )(*(pltpu.with_memory_space_constraint(x, pltpu.HBM) for x in (
            features.reshape(A, C), positions.reshape(3, A), ids.reshape(K, A), counts.reshape(1, A), rw, mix, ro.T,
            rv.reshape(1, H), sw.reshape(1, C))))
        return energy.reshape(1, 1, 1, A), forces.reshape(1, 1, 1, 3, A)

    block = ("gx", "gy", "gz")
    in_specs = (P(*block, None, None),) * 3 + (P(*block, None),) + (P(),) * 5
    out_specs = (P(*block, None), P(*block, None, None))
    return jax.shard_map(body, mesh=mesh, in_specs=in_specs, out_specs=out_specs, check_vma=False)
```
